128 devices in a mesh: rep: 32 (over x, y, core), mp: 4 (over z).
Axes of the slice: x: 4, y: 4, z: 4, core: 2. Of those that a mesh axis runs over, the one named last changes fastest.
Arguments:
- tokens: bfloat16 [16384, 8192], P('rep', 'mp'), may hold values from -6 to 6
- tok_adapter: int32 [16384], P('rep'), may hold values from 0 to 255, as said below
- requests: int32 [32, 32], P('rep'), may hold values from 0 to 255, as said below
- owner_table: int32 [256], replicated, may hold values from 0 to 255, as said below
- q_weight: bfloat16 [8192, 4096], P(None, 'mp'), may hold values from -0.0625 to 0.0625
- pool_a: bfloat16 [256, 64, 8192], P('rep', None, 'mp'), may hold values from -0.0625 to 0.0625
- pool_b: bfloat16 [256, 64, 4096], P('rep', None, 'mp'), may hold values from -0.75 to 0.75
Outputs:
- queries: bfloat16 [16384, 4096], P('rep', 'mp')
The draws below stay inside these ranges and needn't reach their ends.
Inputs may be any that keep to these rules, and one draw needn't show every extreme that they name: owner_table is a permutation of the pool rows; the owner of pool row p is the replica index p // 8. `requests`: each replica's list holds 32 distinct adapter ids; at most 2 of them lie on any one owner, and in every list some owners hold exactly 2. `tok_adapter`: each token's adapter id is one of its own replica's requested ids, and every requested id is named by some token of that replica; at most 62 tokens of one replica name adapters held by one owner, and in every replica some owner gets exactly 62.
All inputs are finite; a program needn't handle non-finite values.
Results may differ from the reference program's by a relative error of at most 0.0039.
Values may be sent and summed in bfloat16 or wider, within the bound.
A program may use at most 256 MiB of HBM per device.

```python
import jax
import jax.numpy as jnp
from jax import lax

D = 8192
OUT = 4096
R = 64
ADP_DEV = 8
TOK_DEV = 512
ADAPTERS = 256
REQ = 32
TOKENS = 16384
N_REP = 32


def pool_plan(key):
    placing = jax.random.permutation(jax.random.fold_in(key, 11), ADAPTERS).astype(jnp.int32)
    quarter = N_REP // 4
    half = REQ // 2
    base = TOK_DEV // N_REP

    def one_list(subkey):
        key_a, key_b, key_c, key_d, key_e = jax.random.split(subkey, 5)
        order = jax.random.permutation(key_a, N_REP).astype(jnp.int32)
        doubles = order[:quarter]
        singles = order[quarter:3 * quarter]
        first = jax.random.randint(key_b, (quarter,), 0, ADP_DEV)
        offset = jax.random.randint(key_c, (quarter,), 1, ADP_DEV)
        second = (first + offset) % ADP_DEV
        alone = jax.random.randint(key_d, (2 * quarter,), 0, ADP_DEV)
        owners = jnp.concatenate([doubles, doubles, singles])
        local_rows = jnp.concatenate([first, second, alone]).astype(jnp.int32)
        pool_rows = (owners * ADP_DEV + local_rows).astype(jnp.int32)
        moved = jax.random.randint(key_e, (half,), 0, base).astype(jnp.int32)
        moved = moved.at[0].set(base - 1).at[quarter].set(base - 1)
        counts_pre = jnp.concatenate([base + moved, base - moved]).astype(jnp.int32)
        shuffle = jax.random.permutation(jax.random.fold_in(subkey, 5), REQ).astype(jnp.int32)
        return (pool_rows[shuffle], pool_rows[0], counts_pre[shuffle])
    list_keys = jax.random.split(jax.random.fold_in(key, 12), N_REP)
    row_lists, first_rows, slot_counts = jax.vmap(one_list)(list_keys)
    target_row = first_rows[0]
    top_id = ADAPTERS - 1
    holder = jnp.argmax((placing == target_row).astype(jnp.int32)).astype(jnp.int32)
    top_row = placing[top_id]
    placing = placing.at[holder].set(top_row)
    placing = placing.at[top_id].set(target_row)
    inverse = jnp.argsort(placing).astype(jnp.int32)
    lists = inverse[row_lists].astype(jnp.int32)
    return (placing, lists, slot_counts)


def draw_owner_table(key, part):
    placing, lists, slot_counts = pool_plan(key)
    return placing


def draw_requests(key, part):
    placing, lists, slot_counts = pool_plan(key)
    return lists


def draw_tok_adapter(key, part):
    placing, lists, slot_counts = pool_plan(key)
    key = jax.random.fold_in(key, 3)
    ends = jnp.cumsum(slot_counts, axis=1).astype(jnp.int32)
    positions = jnp.arange(TOK_DEV, dtype=jnp.int32)
    slots = jnp.sum((positions[None, :, None] >= ends[:, None, :]).astype(jnp.int32), axis=2).astype(jnp.int32)
    row_keys = jax.random.split(key, N_REP)
    orders = jax.vmap(lambda one_key: jax.random.permutation(one_key, TOK_DEV).astype(jnp.int32))(row_keys)
    slots = jnp.take_along_axis(slots, orders, axis=1)
    chosen = jnp.take_along_axis(lists, slots, axis=1)
    return chosen.reshape(TOKENS).astype(jnp.int32)


def steps_of(stream_key, dims, cuts, smallest, top_value):
    def one(position, parts):
        heights = jax.random.uniform(jax.random.fold_in(jax.random.fold_in(stream_key, 6), position), (parts,), jnp.float32, smallest / len(cuts), top_value / len(cuts))
        return jnp.repeat(jnp.exp(heights), dims[position] // parts).reshape((-1,) + (1,) * (len(dims) - position - 1))

    loudness = one(*cuts[0])
    for cut in cuts[1:]:
        loudness = loudness * one(*cut)
    return loudness


def noise(own_key, shape, deviation, limit, pieces=(), kind=jnp.bfloat16):
    level = steps_of(own_key, shape, pieces, -0.22, 0.18) if pieces else 1.0
    entries = jax.random.normal(own_key, shape, jnp.float32) * deviation * level
    return jnp.minimum(jnp.maximum(entries, -limit), limit).astype(kind)


def setup_inputs(seed: int = 0) -> dict:
    key_of = jax.random.split(jax.random.key(seed), 8)
    return {
        "tokens": noise(key_of[0], (TOKENS, D), 1.0, 6.0, ((0, 32), (1, 4))),
        "tok_adapter": draw_tok_adapter(jax.random.fold_in(key_of[7], 71), 0),
        "requests": draw_requests(jax.random.fold_in(key_of[7], 71), 0),
        "owner_table": draw_owner_table(jax.random.fold_in(key_of[7], 71), 0),
        "q_weight": noise(key_of[4], (D, OUT), D ** -0.5, 0.0625, ((1, 4),)),
        "pool_a": noise(key_of[5], (ADAPTERS, R, D), D ** -0.5, 0.0625, ((0, 32), (2, 4))),
        "pool_b": noise(key_of[6], (ADAPTERS, R, OUT), R ** -0.5, 0.75, ((0, 32), (2, 4))),
    }


def reference(tokens, tok_adapter, requests, owner_table, q_weight, pool_a, pool_b):
    groups = tokens.reshape(N_REP, TOK_DEV, D)
    id_groups = tok_adapter.reshape(N_REP, TOK_DEV)

    def one_replica(inputs):
        rows_x, rows_id, wanted = inputs
        pool_rows = owner_table[wanted]
        a_pages = pool_a[pool_rows].reshape(REQ * R, D)
        b_pages = pool_b[pool_rows].reshape(REQ * R, OUT)
        base_out = jnp.dot(rows_x, q_weight, preferred_element_type=jnp.float32)
        shrink = lax.dot_general(rows_x, a_pages, (((1,), (1,)), ((), ())), preferred_element_type=jnp.float32)
        shrink = shrink.reshape(TOK_DEV, REQ, R)
        one_hot = (rows_id[:, None] == wanted[None, :]).astype(jnp.float32)
        rank_vals = jnp.sum(shrink * one_hot[:, :, None], axis=1).astype(jnp.bfloat16)
        spread = (one_hot[:, :, None] * rank_vals.astype(jnp.float32)[:, None, :]).astype(jnp.bfloat16)
        delta = jnp.dot(spread.reshape(TOK_DEV, REQ * R), b_pages, preferred_element_type=jnp.float32)
        return (base_out + delta).astype(jnp.bfloat16)

    result = lax.map(one_replica, (groups, id_groups, requests))
    return result.reshape(TOKENS, OUT)
```

```python
import jax
import jax.numpy as jnp
from jax import lax
from jax.experimental import pallas as pl
from jax.experimental.pallas import tpu as pltpu
from jax.sharding import PartitionSpec as P

MESH = pl.DeviceIdType.MESH
F32 = jnp.float32
BF16 = jnp.bfloat16

OFFS = (
    (0, 0),
    (1, 0), (3, 0), (0, 1), (0, 3),
    (1, 1), (3, 3), (1, 3), (3, 1),
    (2, 1), (1, 2), (2, 3), (3, 2),
    (2, 0), (0, 2), (2, 2),
)
CHIPS = 16
LOW_X = sum(dx << (2 * i) for i, (dx, _) in enumerate(OFFS[:8]))
HIGH_X = sum(dx << (2 * i) for i, (dx, _) in enumerate(OFFS[8:]))
LOW_Y = sum(dy << (2 * i) for i, (_, dy) in enumerate(OFFS[:8]))
HIGH_Y = sum(dy << (2 * i) for i, (_, dy) in enumerate(OFFS[8:]))
NT = (((1,), (1,)), ((), ()))
NN = (((1,), (0,)), ((), ()))


def lookup(values, i):
    found = jnp.int32(0)
    for j, value in enumerate(values):
        if value:
            found = found + value * (i == j).astype(jnp.int32)
    return found


def kernel(
    tokens, meta, table, weight, pool_a, pool_b,
    out,
    full, wts, tok, pages_a, pb_in, pb_send, pages_b, metas, smem, stage,
    part_send, part_recv, zsum, zrecv, ranks, delta_send, delta_recv, acc,
    z_s, z_r, tok_s, tok_r, a_s, a_r, ac_s, ac_r, b_s, b_r, bc_s, bc_r, m_s, m_r,
    p_s, p_r, zp_s, zp_r, zq_s, zq_r, k_s, k_r, d_s, d_r, loc,
):
    rep = lax.axis_index("rep")
    z = lax.axis_index("mp")
    x, y, core = rep // 8, (rep // 2) % 4, rep % 2
    chip = x * 4 + y

    def ahead(i):
        dx, dy = OFFS[i]
        return (((x + dx) % 4) * 4 + (y + dy) % 4) * 2 + core

    def behind(i):
        dx, dy = OFFS[i]
        return (((x + 4 - dx) % 4) * 4 + (y + 4 - dy) % 4) * 2 + core

    def behind_loop(i):
        dx = lookup([o[0] for o in OFFS], i)
        dy = lookup([o[1] for o in OFFS], i)
        return (((x + 4 - dx) % 4) * 4 + (y + 4 - dy) % 4) * 2 + core

    def zat(d):
        return (z + d) % 4

    sibling = rep + 1 - 2 * core

    def remote(src, dst, ss, rs, dev):
        return pltpu.make_async_remote_copy(
            src_ref=src, dst_ref=dst, send_sem=ss, recv_sem=rs, device_id=dev, device_id_type=MESH
        )

    local = [
        pltpu.make_async_copy(tokens, full.at[z], loc.at[0]),
        pltpu.make_async_copy(pool_b, pb_in, loc.at[1]),
        pltpu.make_async_copy(tokens.at[:, pl.ds(chip * 128, 128)], tok.at[0], loc.at[2]),
        pltpu.make_async_copy(
            pool_a.at[:, :, pl.ds(chip * 128, 128)], pages_a.at[pl.ds(rep * 8, 8)], loc.at[3]
        ),
    ]
    wloads = [
        pltpu.make_async_copy(weight.at[pl.ds(zat(d) * 2048, 2048)], wts.at[d], loc.at[4 + d])
        for d in range(4)
    ]

    barrier = pltpu.get_barrier_semaphore()
    for i in range(1, CHIPS):
        pl.semaphore_signal(barrier, inc=1, device_id=(ahead(i), z), device_id_type=MESH)
    pl.semaphore_signal(barrier, inc=1, device_id=(sibling, z), device_id_type=MESH)
    for d in range(1, 4):
        pl.semaphore_signal(barrier, inc=1, device_id=(rep, zat(d)), device_id_type=MESH)
    for copy in (local[1], local[0], local[2], local[3], wloads[0], wloads[3], wloads[1], wloads[2]):
        copy.start()
    metas[0] = meta[...]
    pl.semaphore_wait(barrier, CHIPS - 1 + 4)

    def rows(c):
        return pl.ds(c * 128, 128)

    def z_own(way, c):
        dev = (rep, zat(1 if way == 0 else 3))
        return remote(tokens.at[rows(c)], full.at[z, rows(c)], z_s.at[way, c], z_r.at[way, c], dev)

    def z_relay(way, n):
        c = n + 2 * way
        src = zat(3 if way == 0 else 1)
        dev = (rep, zat(1 if way == 0 else 3))
        part = full.at[src, rows(c)]
        return remote(part, part, z_s.at[way, 4 + n], z_r.at[way, 4 + n], dev)

    for n in range(4):
        z_own(0, n).start()
        z_own(1, (n + 2) % 4).start()

    def send_meta(i):
        return remote(meta, metas.at[i], m_s.at[i], m_r.at[i], (ahead(i), z))

    def send_a(i):
        to = ahead(i)
        return remote(
            pool_a.at[:, :, pl.ds((to // 2) * 128, 128)], pages_a.at[pl.ds(rep * 8, 8)],
            a_s.at[i], a_r.at[i], (to, z),
        )

    def send_tok(i):
        to = ahead(i)
        return remote(
            tokens.at[:, pl.ds((to // 2) * 128, 128)], tok.at[i], tok_s.at[i], tok_r.at[i], (to, z)
        )

    def send_b(i):
        to = ahead(i)
        return remote(
            pb_send.at[to // 2], pages_b.at[pl.ds(rep * 4, 4)], b_s.at[i], b_r.at[i], (to, z)
        )

    for i in range(1, CHIPS):
        send_a(i).start()
    for i in range(1, CHIPS):
        send_meta(i).start()
    for i in range(1, CHIPS):
        send_tok(i).start()

    local[1].wait()

    @pl.loop(0, 4)
    def _(q):
        for j in range(8):
            block = pb_in[q, :, j * 128 : (j + 1) * 128].astype(F32).T.astype(BF16)
            pb_send[2 * j, q] = block[:64]
            pb_send[2 * j + 1, q] = block[64:]

    pages_b[pl.ds(rep * 4, 4)] = pb_send[chip]
    for i in range(1, CHIPS):
        send_b(i).start()

    def base_block(d, first):
        m = zat(d)

        @pl.loop(0, 4)
        def _(n):
            cols = pl.ds(pl.multiple_of(n * 256, 256), 256)
            term = jnp.dot(full[m], wts[d, :, cols], preferred_element_type=F32)
            if first:
                acc[:, cols] = term
            else:
                acc[:, cols] += term

    local[0].wait()
    wloads[0].wait()
    base_block(0, True)

    def relay_a(i):
        owner = behind(i)
        piece = pages_a.at[pl.ds(owner * 8, 8)]
        return remote(piece, piece, ac_s.at[i], ac_r.at[i], (sibling, z))

    def relay_b(i):
        owner = behind(i)
        piece = pages_b.at[pl.ds(owner * 4, 4)]
        return remote(piece, piece, bc_s.at[i], bc_r.at[i], (sibling, z))

    local[3].wait()
    relay_a(0).start()
    relay_b(0).start()
    for i in range(1, CHIPS):
        send_a(i).wait_recv()
        relay_a(i).start()
        if i == 8:
            for n in range(2):
                z_own(0, n).wait_recv()
                z_relay(0, n).start()
                z_own(1, n + 2).wait_recv()
                z_relay(1, n).start()
    for i in range(1, CHIPS):
        send_meta(i).wait_recv()
    smem_copy = pltpu.make_async_copy(metas, smem, loc.at[8])
    smem_copy.start()
    for i in range(CHIPS):
        relay_a(i).wait_recv()
    smem_copy.wait()

    def half_ids(i, h):
        own = metas[i]
        return jnp.concatenate([own[4 + 2 * h : 5 + 2 * h], own[5 + 2 * h : 6 + 2 * h]], axis=1)

    def shrink(i):
        for s in range(32):
            stage[s * 64 : (s + 1) * 64] = pages_a[table[smem[i, 0, s]]]
        for h in range(2):
            ids = half_ids(i, h)
            feats = tok[i, h * 256 : (h + 1) * 256]
            total = jnp.zeros((64, 256), F32)
            for g in range(4):
                got = lax.dot_general(
                    stage[g * 512 : (g + 1) * 512], feats, NT, preferred_element_type=F32
                )
                for s in range(8):
                    hit = ids == smem[i, 0, g * 8 + s]
                    total = jnp.where(hit, got[s * 64 : (s + 1) * 64], total)
            part_send[i, :, h * 256 : (h + 1) * 256] = total

    def send_part(i, dev):
        return remote(part_send.at[i], part_recv.at[i], p_s.at[i], p_r.at[i], (dev, z))

    local[2].wait()

    @pl.loop(0, CHIPS)
    def _(i):
        @pl.when(i > 0)
        def _():
            remote(tok.at[i], tok.at[i], tok_s.at[i], tok_r.at[i], (rep, zat(1))).wait_recv()

        shrink(i)

        @pl.when(i > 0)
        def _():
            send_part(i, behind_loop(i)).start()

    for n in range(4):
        if n >= 2:
            z_own(0, n).wait_recv()
            z_own(1, (n + 2) % 4).wait_recv()
    wloads[3].wait()
    base_block(3, False)
    wloads[1].wait()
    base_block(1, False)

    for i in range(1, CHIPS):
        send_b(i).wait_recv()
        relay_b(i).start()

    for i in range(1, CHIPS):
        send_part(i, rep).wait_recv()
    for q in range(4):
        cols = slice(q * 128, (q + 1) * 128)
        total = part_send[0, :, cols]
        for i in range(1, CHIPS):
            total = total + part_recv[i, :, cols]
        zsum[q] = total

    def send_zsum(d):
        to = zat(d)
        return remote(zsum.at[to], zrecv.at[d], zp_s.at[d], zp_r.at[d], (rep, to))

    for d in (2, 1, 3):
        send_zsum(d).start()
    for d in range(1, 4):
        send_zsum(d).wait_recv()
    ranks[0, z] = (zsum[z] + zrecv[1] + zrecv[2] + zrecv[3]).astype(BF16)

    def send_quarter(d):
        part = ranks.at[0, z]
        return remote(part, part, zq_s.at[d], zq_r.at[d], (rep, zat(d)))

    for d in (2, 1, 3):
        send_quarter(d).start()
    for d in range(1, 4):
        send_quarter(d).wait_recv()

    def send_rank(i):
        return remote(ranks.at[0], ranks.at[i], k_s.at[i], k_r.at[i], (ahead(i), z))

    for i in range(1, CHIPS):
        send_rank(i).start()
    for i in range(CHIPS):
        relay_b(i).wait_recv()

    def expand(i):
        for s in range(32):
            stage[s * 64 : (s + 1) * 64] = pages_b[table[smem[i, 0, s]] // 2]
        for h in range(2):
            ids = half_ids(i, h)
            odd = jnp.zeros((1, 256), jnp.int32)
            for s in range(32):
                name = smem[i, 0, s]
                odd = jnp.where(ids == name, table[name] % 2, odd)
            vals = jnp.concatenate([ranks[i, 2 * h], ranks[i, 2 * h + 1]], axis=1).astype(F32)
            vals = jnp.concatenate(
                [jnp.where(odd == 0, vals, 0.0), jnp.where(odd == 1, vals, 0.0)], axis=0
            ).astype(BF16)
            total = jnp.zeros((64, 256), F32)
            for g in range(4):
                got = lax.dot_general(
                    stage[g * 512 : (g + 1) * 512], vals, NN, preferred_element_type=F32
                )
                for s in range(8):
                    hit = ids == smem[i, 0, g * 8 + s]
                    total = jnp.where(hit, got[s * 64 : (s + 1) * 64], total)
            delta_send[i, :, h * 256 : (h + 1) * 256] = total.astype(BF16)

    def send_delta(i, dev):
        return remote(delta_send.at[i], delta_recv.at[chip], d_s.at[i], d_r.at[i], (dev, z))

    @pl.loop(0, CHIPS)
    def _(i):
        @pl.when(i > 0)
        def _():
            remote(ranks.at[i], ranks.at[i], k_s.at[i], k_r.at[i], (rep, zat(1))).wait_recv()

        expand(i)

        @pl.when(i > 0)
        def _():
            send_delta(i, behind_loop(i)).start()

    delta_recv[chip] = delta_send[0]

    for n in range(2):
        z_relay(0, n).wait_recv()
        z_relay(1, n).wait_recv()
    wloads[2].wait()
    base_block(2, False)

    for i in range(1, CHIPS):
        send_delta(i, rep).wait_recv()

    @pl.loop(0, 8)
    def _(j):
        cols = pl.ds(pl.multiple_of(j * 128, 128), 128)
        block = jnp.concatenate([delta_recv[2 * j], delta_recv[2 * j + 1]], axis=0)
        out[:, cols] = (acc[:, cols] + block.astype(F32).T).astype(BF16)

    for way in range(2):
        for n in range(4):
            z_own(way, n).wait_send()
        for n in range(2):
            z_relay(way, n).wait_send()
    for i in range(1, CHIPS):
        send_a(i).wait_send()
        send_meta(i).wait_send()
        send_tok(i).wait_send()
        send_b(i).wait_send()
        send_part(i, rep).wait_send()
        send_rank(i).wait_send()
        send_delta(i, rep).wait_send()
    for i in range(CHIPS):
        relay_a(i).wait_send()
        relay_b(i).wait_send()
    for d in range(1, 4):
        send_zsum(d).wait_send()
        send_quarter(d).wait_send()


def per_device(tokens, tok_adapter, requests, owner_table, q_weight, pool_a, pool_b):
    lists = jnp.pad(requests, ((0, 3), (0, 96)))
    meta = jnp.concatenate([lists, tok_adapter.reshape(4, 128)], axis=0)
    dma = pltpu.SemaphoreType.DMA
    anywhere = pl.BlockSpec(memory_space=pl.ANY)
    vmem = pl.BlockSpec(memory_space=pltpu.VMEM)
    smem = pl.BlockSpec(memory_space=pltpu.SMEM)
    return pl.pallas_call(
        kernel,
        out_shape=jax.ShapeDtypeStruct((512, 1024), BF16),
        in_specs=[anywhere, vmem, smem, anywhere, anywhere, anywhere],
        out_specs=vmem,
        scratch_shapes=[
            pltpu.VMEM((4, 512, 2048), BF16),
            pltpu.VMEM((4, 2048, 1024), BF16),
            pltpu.VMEM((16, 512, 128), BF16),
            pltpu.VMEM((256, 64, 128), BF16),
            pltpu.VMEM((4, 128, 1024), BF16),
            pltpu.VMEM((16, 4, 64, 128), BF16),
            pltpu.VMEM((128, 64, 128), BF16),
            pltpu.VMEM((16, 8, 128), jnp.int32),
            pltpu.SMEM((16, 8, 128), jnp.int32),
            pltpu.VMEM((2048, 128), BF16),
            pltpu.VMEM((16, 64, 512), F32),
            pltpu.VMEM((16, 64, 512), F32),
            pltpu.VMEM((4, 64, 128), F32),
            pltpu.VMEM((4, 64, 128), F32),
            pltpu.VMEM((16, 4, 64, 128), BF16),
            pltpu.VMEM((16, 64, 512), BF16),
            pltpu.VMEM((16, 64, 512), BF16),
            pltpu.VMEM((512, 1024), F32),
            dma((2, 6)), dma((2, 6)),
            dma((16,)), dma((16,)),
            dma((16,)), dma((16,)),
            dma((16,)), dma((16,)),
            dma((16,)), dma((16,)),
            dma((16,)), dma((16,)),
            dma((16,)), dma((16,)),
            dma((16,)), dma((16,)),
            dma((4,)), dma((4,)),
            dma((4,)), dma((4,)),
            dma((16,)), dma((16,)),
            dma((16,)), dma((16,)),
            dma((9,)),
        ],
        compiler_params=pltpu.CompilerParams(
            collective_id=1, has_side_effects=True, vmem_limit_bytes=62 * 2**20
        ),
        cost_estimate=pl.CostEstimate(
            flops=20_000_000_000, bytes_accessed=30_000_000, transcendentals=0
        ),
        name="lora_projection",
    )(tokens, meta, owner_table, q_weight, pool_a, pool_b.reshape(4, 128, 1024))


def solution(mesh):
    in_specs = (
        P("rep", "mp"),
        P("rep"),
        P("rep", None),
        P(),
        P(None, "mp"),
        P("rep", None, "mp"),
        P("rep", None, "mp"),
    )
    out_specs = P("rep", "mp")
    return jax.shard_map(
        per_device, mesh=mesh, in_specs=in_specs, out_specs=out_specs, check_vma=False
    )
```

```python
import jax
import jax.numpy as jnp
from jax import lax
from jax.experimental import pallas as pl
from jax.experimental.pallas import tpu as pltpu
from jax.sharding import PartitionSpec as P

MESH = pl.DeviceIdType.MESH
F32 = jnp.float32
BF16 = jnp.bfloat16

OFFS = (
    (0, 0),
    (1, 0), (3, 0), (0, 1), (0, 3),
    (1, 1), (3, 3), (1, 3), (3, 1),
    (2, 1), (1, 2), (2, 3), (3, 2),
    (2, 0), (0, 2), (2, 2),
)
CHIPS = 16
NT = (((1,), (1,)), ((), ()))
NN = (((1,), (0,)), ((), ()))


def lookup(values, i):
    found = jnp.int32(0)
    for j, value in enumerate(values):
        if value:
            found = found + value * (i == j).astype(jnp.int32)
    return found


def kernel(
    tokens, meta, table, weight, pool_a, pool_b,
    out,
    full, wts, own_tok, tok, pages_a, pb_in, pb_send, pages_b, metas, smem, pair, odds, stage,
    part_send, part_recv, mid, end, zsum, zrecv, ranks, delta_send, delta_recv, acc,
    z_s, z_r, tok_s, tok_r, a_s, a_r, ac_s, ac_r, b_s, b_r, bc_s, bc_r, m_s, m_r,
    px_s, px_r, py_s, py_r, ex_s, ex_r, ey_s, ey_r, zp_s, zp_r, zq_s, zq_r, k_s, k_r, d_s, d_r, loc,
):
    rep = lax.axis_index("rep")
    z = lax.axis_index("mp")
    x, y, core = rep // 8, (rep // 2) % 4, rep % 2
    chip = x * 4 + y

    def rep_at(cx, cy):
        return (cx * 4 + cy) * 2 + core

    def ahead(i):
        dx, dy = OFFS[i]
        return (((x + dx) % 4) * 4 + (y + dy) % 4) * 2 + core

    def behind(i):
        dx, dy = OFFS[i]
        return (((x + 4 - dx) % 4) * 4 + (y + 4 - dy) % 4) * 2 + core

    def ahead_loop(i):
        dx = lookup([o[0] for o in OFFS], i)
        dy = lookup([o[1] for o in OFFS], i)
        return (((x + dx) % 4) * 4 + (y + dy) % 4) * 2 + core

    def behind_loop(i):
        dx = lookup([o[0] for o in OFFS], i)
        dy = lookup([o[1] for o in OFFS], i)
        return (((x + 4 - dx) % 4) * 4 + (y + 4 - dy) % 4) * 2 + core

    def zat(d):
        return (z + d) % 4

    sibling = rep + 1 - 2 * core

    def remote(src, dst, ss, rs, dev):
        return pltpu.make_async_remote_copy(
            src_ref=src, dst_ref=dst, send_sem=ss, recv_sem=rs, device_id=dev, device_id_type=MESH
        )

    local = [
        pltpu.make_async_copy(tokens, full.at[z], loc.at[0]),
        pltpu.make_async_copy(pool_b, pb_in, loc.at[1]),
        pltpu.make_async_copy(tokens.at[:, pl.ds(chip * 128, 128)], own_tok, loc.at[2]),
        pltpu.make_async_copy(
            pool_a.at[:, :, pl.ds(chip * 128, 128)], pages_a.at[pl.ds(rep * 8, 8)], loc.at[3]
        ),
    ]
    wloads = [
        pltpu.make_async_copy(weight.at[pl.ds(zat(d) * 2048, 2048)], wts.at[d], loc.at[4 + d])
        for d in range(4)
    ]

    barrier = pltpu.get_barrier_semaphore()
    for i in range(1, CHIPS):
        pl.semaphore_signal(barrier, inc=1, device_id=(ahead(i), z), device_id_type=MESH)
    pl.semaphore_signal(barrier, inc=1, device_id=(sibling, z), device_id_type=MESH)
    for d in range(1, 4):
        pl.semaphore_signal(barrier, inc=1, device_id=(rep, zat(d)), device_id_type=MESH)
    for copy in (local[1], local[0], local[2], local[3], wloads[0], wloads[3], wloads[1], wloads[2]):
        copy.start()
    metas[0] = meta[...]
    pl.semaphore_wait(barrier, CHIPS - 1 + 4)

    def rows(c):
        return pl.ds(c * 128, 128)

    def z_own(way, c):
        dev = (rep, zat(1 if way == 0 else 3))
        return remote(tokens.at[rows(c)], full.at[z, rows(c)], z_s.at[way, c], z_r.at[way, c], dev)

    def z_relay(way, n):
        c = n + 2 * way
        src = zat(3 if way == 0 else 1)
        dev = (rep, zat(1 if way == 0 else 3))
        part = full.at[src, rows(c)]
        return remote(part, part, z_s.at[way, 4 + n], z_r.at[way, 4 + n], dev)

    def send_meta(i):
        return remote(meta, metas.at[i], m_s.at[i], m_r.at[i], (ahead(i), z))

    def send_a(i):
        to = ahead(i)
        return remote(
            pool_a.at[:, :, pl.ds((to // 2) * 128, 128)], pages_a.at[pl.ds(rep * 8, 8)],
            a_s.at[i], a_r.at[i], (to, z),
        )

    def send_tok(half, i, to):
        n = half * CHIPS + i
        start = pl.multiple_of((to // 2) * 128, 128)
        return remote(
            tokens.at[pl.ds(half * 256, 256), pl.ds(start, 128)], tok.at[half, i],
            tok_s.at[n], tok_r.at[n], (to, z),
        )

    def send_b(i):
        to = ahead(i)
        return remote(
            pb_send.at[to // 2], pages_b.at[pl.ds(rep * 4, 4)], b_s.at[i], b_r.at[i], (to, z)
        )

    def relay_a(i):
        piece = pages_a.at[pl.ds(behind(i) * 8, 8)]
        return remote(piece, piece, ac_s.at[i], ac_r.at[i], (sibling, z))

    def relay_b(i):
        piece = pages_b.at[pl.ds(behind(i) * 4, 4)]
        return remote(piece, piece, bc_s.at[i], bc_r.at[i], (sibling, z))

    for i in range(1, CHIPS):
        send_a(i).start()
    for n in range(2):
        z_own(0, n).start()
        z_own(1, n + 2).start()
    for i in range(1, CHIPS):
        send_meta(i).start()
    for i in range(1, CHIPS):
        send_tok(0, i, ahead(i)).start()

    local[1].wait()

    @pl.loop(0, 4)
    def _(q):
        for j in range(8):
            block = pb_in[q, :, j * 128 : (j + 1) * 128].astype(F32).T.astype(BF16)
            pb_send[2 * j, q] = block[:64]
            pb_send[2 * j + 1, q] = block[64:]

    pages_b[pl.ds(rep * 4, 4)] = pb_send[chip]

    def base_block(d, first):
        m = zat(d)

        @pl.loop(0, 4)
        def _(n):
            cols = pl.ds(pl.multiple_of(n * 256, 256), 256)
            term = jnp.dot(full[m], wts[d, :, cols], preferred_element_type=F32)
            if first:
                acc[:, cols] = term
            else:
                acc[:, cols] += term

    local[3].wait()
    relay_a(0).start()
    relay_b(0).start()
    local[0].wait()
    wloads[0].wait()
    base_block(0, True)

    for i in range(1, CHIPS):
        send_a(i).wait_recv()
        relay_a(i).start()
        send_tok(1, i, ahead(i)).start()
    for n in range(2):
        z_own(0, n + 2).start()
        z_own(1, n).start()
    for i in range(1, CHIPS):
        send_meta(i).wait_recv()
    smem_copy = pltpu.make_async_copy(metas, smem, loc.at[8])
    smem_copy.start()
    for i in range(CHIPS):
        relay_a(i).wait_recv()
    smem_copy.wait()
    local[2].wait()
    tok[0, 0] = own_tok[:256]
    tok[1, 0] = own_tok[256:]

    def ids_of(i, half):
        own = metas[i]
        first = 4 + 2 * half
        return jnp.concatenate([own[first : first + 1], own[first + 1 : first + 2]], axis=1)

    def by_slot(i, ids, left, right, dims):
        total = jnp.zeros((64, 256), F32)
        for g in range(4):
            got = lax.dot_general(
                left[g * 512 : (g + 1) * 512], right, dims, preferred_element_type=F32
            )
            for s in range(8):
                hit = ids == smem[i, 0, g * 8 + s]
                total = jnp.where(hit, got[s * 64 : (s + 1) * 64], total)
        return total

    def send_px(half, i, dev):
        n = half * CHIPS + i
        rows = pl.ds(0, 32)
        return remote(
            part_send.at[half, i, rows], part_recv.at[half, i, rows], px_s.at[n], px_r.at[n],
            (dev, z),
        )

    def send_py(half, i, dev):
        n = half * CHIPS + i
        rows = pl.ds(32, 32)
        return remote(
            part_send.at[half, i, rows], part_recv.at[half, i, rows], py_s.at[n], py_r.at[n],
            (dev, z),
        )

    def shrink(half):
        @pl.loop(0, CHIPS)
        def _(i):
            @pl.when(i > 0)
            def _():
                send_tok(half, i, rep).wait_recv()

            for s in range(32):
                stage[s * 64 : (s + 1) * 64] = pages_a[table[smem[i, 0, s]]]
            part_send[half, i] = by_slot(i, ids_of(i, half), stage, tok[half, i], NT)

            dx = lookup([o[0] for o in OFFS], i)
            dy = lookup([o[1] for o in OFFS], i)

            @pl.when(dx > 0)
            def _():
                send_px(half, i, rep_at((x + 4 - dx) % 4, y)).start()

            @pl.when(dy > 0)
            def _():
                send_py(half, i, rep_at(x, (y + 4 - dy) % 4)).start()

    shrink(0)
    for n in range(2):
        z_own(0, n).wait_recv()
        z_relay(0, n).start()
        z_own(1, n + 2).wait_recv()
        z_relay(1, n).start()
    shrink(1)

    def send_ex(half, dy):
        n = half * 4 + dy
        dev = rep_at(x, (y + 4 - dy) % 4)
        return remote(mid.at[half, 0, dy], end.at[half, 0, dy], ex_s.at[n], ex_r.at[n], (dev, z))

    def send_ey(half, dx):
        n = half * 4 + dx
        dev = rep_at((x + 4 - dx) % 4, y)
        return remote(mid.at[half, 1, dx], end.at[half, 1, dx], ey_s.at[n], ey_r.at[n], (dev, z))

    def first_sums(half):
        for o in (1, 3, 2, 0):
            for d in range(1, 4):
                send_px(half, OFFS.index((d, o)), rep).wait_recv()
            total = part_send[half, OFFS.index((0, o)), :32]
            for d in range(1, 4):
                total = total + part_recv[half, OFFS.index((d, o)), :32]
            mid[half, 0, o] = total
            if o:
                send_ex(half, o).start()
            for d in range(1, 4):
                send_py(half, OFFS.index((o, d)), rep).wait_recv()
            total = part_send[half, OFFS.index((o, 0)), 32:]
            for d in range(1, 4):
                total = total + part_recv[half, OFFS.index((o, d)), 32:]
            mid[half, 1, o] = total
            if o:
                send_ey(half, o).start()

    def collect(half):
        for axis in range(2):
            total = mid[half, axis, 0]
            for o in (1, 3, 2):
                (send_ey if axis else send_ex)(half, o).wait_recv()
                total = total + end[half, axis, o]
            zsum[half, 2 * axis] = total[:16]
            zsum[half, 2 * axis + 1] = total[16:]

    def send_zsum(half, d):
        to = zat(d)
        n = half * 4 + d
        return remote(zsum.at[half, to], zrecv.at[half, d], zp_s.at[n], zp_r.at[n], (rep, to))

    def start_sums(half):
        for d in (2, 1, 3):
            send_zsum(half, d).start()

    def send_rank(half, i, to):
        n = half * CHIPS + i
        return remote(ranks.at[half, z, 0], ranks.at[half, z, i], k_s.at[n], k_r.at[n], (to, z))

    def pass_rank(half, g, d):
        n = (half * 4 + g) * 4 + d
        part = ranks.at[half, z, pl.ds(g * 4, 4)]
        return remote(part, part, zq_s.at[n], zq_r.at[n], (rep, zat(d)))

    def start_ranks(half):
        for d in range(1, 4):
            send_zsum(half, d).wait_recv()
        ranks[half, z, 0] = (
            zsum[half, z] + zrecv[half, 1] + zrecv[half, 2] + zrecv[half, 3]
        ).astype(BF16)
        for i in range(1, CHIPS):
            send_rank(half, i, ahead(i)).start()

    def pass_ranks(half):
        for g in range(4):
            for i in range(max(1, 4 * g), 4 * g + 4):
                send_rank(half, i, rep).wait_recv()
            for d in (2, 1, 3):
                pass_rank(half, g, d).start()

    @pl.loop(0, CHIPS)
    def _(i):
        ids = jnp.concatenate([ids_of(i, 0), ids_of(i, 1)], axis=1)
        odd = jnp.zeros((1, 512), jnp.int32)
        for s in range(32):
            name = smem[i, 0, s]
            page = table[name]
            pair[i, s] = page >> 1
            odd = jnp.where(ids == name, page & 1, odd)
        odds[i] = odd

    first_sums(0)
    collect(0)
    start_sums(0)
    first_sums(1)
    for i in range(1, CHIPS):
        send_b(i).start()
    start_ranks(0)
    collect(1)
    start_sums(1)
    for n in range(2):
        z_own(0, n + 2).wait_recv()
    wloads[3].wait()
    base_block(3, False)
    start_ranks(1)
    pass_ranks(0)
    pass_ranks(1)
    for n in range(2):
        z_own(1, n).wait_recv()
    wloads[1].wait()
    for i in range(1, CHIPS):
        send_b(i).wait_recv()
        relay_b(i).start()
    base_block(1, False)
    for i in range(CHIPS):
        relay_b(i).wait_recv()

    def send_delta(i, dev):
        return remote(delta_send.at[i], delta_recv.at[chip], d_s.at[i], d_r.at[i], (dev, z))

    @pl.loop(0, CHIPS)
    def _(i):
        for s in range(32):
            stage[s * 64 : (s + 1) * 64] = pages_b[pair[i, s]]

        @pl.when(i % 4 == 0)
        def _():
            for half in range(2):
                for d in range(1, 4):
                    pass_rank(half, i // 4, d).wait_recv()

        for half in range(2):
            odd = odds[i, :, half * 256 : (half + 1) * 256]
            vals = jnp.concatenate([ranks[half, q, i] for q in range(4)], axis=0).astype(F32)
            vals = jnp.concatenate(
                [jnp.where(odd == 0, vals, 0.0), jnp.where(odd == 1, vals, 0.0)], axis=0
            ).astype(BF16)
            delta_send[i, half] = by_slot(i, ids_of(i, half), stage, vals, NN).astype(BF16)

        @pl.when(i > 0)
        def _():
            send_delta(i, behind_loop(i)).start()

    delta_recv[chip] = delta_send[0]

    for n in range(2):
        z_relay(0, n).wait_recv()
        z_relay(1, n).wait_recv()
    wloads[2].wait()
    base_block(2, False)

    for i in range(1, CHIPS):
        send_delta(i, rep).wait_recv()
    for half in range(2):

        @pl.loop(0, 8)
        def _(j):
            part = pl.ds(half * 256, 256)
            cols = pl.ds(pl.multiple_of(j * 128, 128), 128)
            block = jnp.concatenate(
                [delta_recv[2 * j, half], delta_recv[2 * j + 1, half]], axis=0
            )
            out[part, cols] = (acc[part, cols] + block.astype(F32).T).astype(BF16)

    for way in range(2):
        for n in range(4):
            z_own(way, n).wait_send()
        for n in range(2):
            z_relay(way, n).wait_send()
    for i in range(1, CHIPS):
        send_a(i).wait_send()
        send_meta(i).wait_send()
        send_b(i).wait_send()
        send_delta(i, rep).wait_send()
        for half in range(2):
            send_tok(half, i, rep).wait_send()
            send_rank(half, i, rep).wait_send()
    for i in range(CHIPS):
        relay_a(i).wait_send()
        relay_b(i).wait_send()
    for half in range(2):
        for i, (dx, dy) in enumerate(OFFS):
            if dx:
                send_px(half, i, rep).wait_send()
            if dy:
                send_py(half, i, rep).wait_send()
        for d in range(1, 4):
            send_ex(half, d).wait_send()
            send_ey(half, d).wait_send()
            send_zsum(half, d).wait_send()
            for g in range(4):
                pass_rank(half, g, d).wait_send()


def per_device(tokens, tok_adapter, requests, owner_table, q_weight, pool_a, pool_b):
    lists = jnp.pad(requests, ((0, 3), (0, 96)))
    meta = jnp.concatenate([lists, tok_adapter.reshape(4, 128)], axis=0)
    dma = pltpu.SemaphoreType.DMA
    anywhere = pl.BlockSpec(memory_space=pl.ANY)
    vmem = pl.BlockSpec(memory_space=pltpu.VMEM)
    smem = pl.BlockSpec(memory_space=pltpu.SMEM)
    return pl.pallas_call(
        kernel,
        out_shape=jax.ShapeDtypeStruct((512, 1024), BF16),
        in_specs=[anywhere, vmem, smem, anywhere, anywhere, anywhere],
        out_specs=vmem,
        scratch_shapes=[
            pltpu.VMEM((4, 512, 2048), BF16),
            pltpu.VMEM((4, 2048, 1024), BF16),
            pltpu.VMEM((512, 128), BF16),
            pltpu.VMEM((2, 16, 256, 128), BF16),
            pltpu.VMEM((256, 64, 128), BF16),
            pltpu.VMEM((4, 128, 1024), BF16),
            pltpu.VMEM((16, 4, 64, 128), BF16),
            pltpu.VMEM((128, 64, 128), BF16),
            pltpu.VMEM((16, 8, 128), jnp.int32),
            pltpu.SMEM((16, 8, 128), jnp.int32),
            pltpu.SMEM((16, 32), jnp.int32),
            pltpu.VMEM((16, 1, 512), jnp.int32),
            pltpu.VMEM((2048, 128), BF16),
            pltpu.VMEM((2, 16, 64, 256), F32),
            pltpu.VMEM((2, 16, 64, 256), F32),
            pltpu.VMEM((2, 2, 4, 32, 256), F32),
            pltpu.VMEM((2, 2, 4, 32, 256), F32),
            pltpu.VMEM((2, 4, 16, 256), F32),
            pltpu.VMEM((2, 4, 16, 256), F32),
            pltpu.VMEM((2, 4, 16, 16, 256), BF16),
            pltpu.VMEM((16, 2, 64, 256), BF16),
            pltpu.VMEM((16, 2, 64, 256), BF16),
            pltpu.VMEM((512, 1024), F32),
            dma((2, 6)), dma((2, 6)),
            dma((32,)), dma((32,)),
            dma((16,)), dma((16,)),
            dma((16,)), dma((16,)),
            dma((16,)), dma((16,)),
            dma((16,)), dma((16,)),
            dma((16,)), dma((16,)),
            dma((32,)), dma((32,)),
            dma((32,)), dma((32,)),
            dma((8,)), dma((8,)),
            dma((8,)), dma((8,)),
            dma((8,)), dma((8,)),
            dma((32,)), dma((32,)),
            dma((32,)), dma((32,)),
            dma((16,)), dma((16,)),
            dma((9,)),
        ],
        compiler_params=pltpu.CompilerParams(
            collective_id=1, has_side_effects=True, vmem_limit_bytes=62 * 2**20
        ),
        cost_estimate=pl.CostEstimate(
            flops=20_000_000_000, bytes_accessed=30_000_000, transcendentals=0
        ),
        name="lora_projection",
    )(tokens, meta, owner_table, q_weight, pool_a, pool_b.reshape(4, 128, 1024))


def solution(mesh):
    in_specs = (
        P("rep", "mp"),
        P("rep"),
        P("rep", None),
        P(),
        P(None, "mp"),
        P("rep", None, "mp"),
        P("rep", None, "mp"),
    )
    out_specs = P("rep", "mp")
    return jax.shard_map(
        per_device, mesh=mesh, in_specs=in_specs, out_specs=out_specs, check_vma=False
    )
```

```python
import jax
import jax.numpy as jnp
from jax import lax
from jax.experimental import pallas as pl
from jax.experimental.pallas import tpu as pltpu
from jax.sharding import PartitionSpec as P

MESH = pl.DeviceIdType.MESH
F32 = jnp.float32
BF16 = jnp.bfloat16

OFFS = (
    (0, 0),
    (1, 0), (3, 0), (0, 1), (0, 3),
    (1, 1), (3, 3), (1, 3), (3, 1),
    (2, 1), (1, 2), (2, 3), (3, 2),
    (2, 0), (0, 2), (2, 2),
)
CHIPS = 16
NT = (((1,), (1,)), ((), ()))
NN = (((1,), (0,)), ((), ()))


def lookup(values, i):
    found = jnp.int32(0)
    for j, value in enumerate(values):
        if value:
            found = found + value * (i == j).astype(jnp.int32)
    return found


def kernel(
    tokens, ids_in, list_in, table, weight, pool_a, pool_b,
    out,
    full, wts, own_tok, tok, pages_a, pb_in, pb_send, pages_b, metas, smem, pair, odds, stage,
    part_send, part_recv, mid, end, zsum, zrecv, ranks, delta_send, delta_recv, acc,
    z_s, z_r, tok_s, tok_r, a_s, a_r, ac_s, ac_r, b_s, b_r, bc_s, bc_r, m_s, m_r,
    px_s, px_r, py_s, py_r, ex_s, ex_r, ey_s, ey_r, zp_s, zp_r, zq_s, zq_r, k_s, k_r, d_s, d_r, loc,
):
    rep = lax.axis_index("rep")
    z = lax.axis_index("mp")
    x, y, core = rep // 8, (rep // 2) % 4, rep % 2
    chip = x * 4 + y

    def rep_at(cx, cy):
        return (cx * 4 + cy) * 2 + core

    def ahead(i):
        dx, dy = OFFS[i]
        return (((x + dx) % 4) * 4 + (y + dy) % 4) * 2 + core

    def behind(i):
        dx, dy = OFFS[i]
        return (((x + 4 - dx) % 4) * 4 + (y + 4 - dy) % 4) * 2 + core

    def ahead_loop(i):
        dx = lookup([o[0] for o in OFFS], i)
        dy = lookup([o[1] for o in OFFS], i)
        return (((x + dx) % 4) * 4 + (y + dy) % 4) * 2 + core

    def behind_loop(i):
        dx = lookup([o[0] for o in OFFS], i)
        dy = lookup([o[1] for o in OFFS], i)
        return (((x + 4 - dx) % 4) * 4 + (y + 4 - dy) % 4) * 2 + core

    def zat(d):
        return (z + d) % 4

    sibling = rep + 1 - 2 * core

    def remote(src, dst, ss, rs, dev):
        return pltpu.make_async_remote_copy(
            src_ref=src, dst_ref=dst, send_sem=ss, recv_sem=rs, device_id=dev, device_id_type=MESH
        )

    local = [
        pltpu.make_async_copy(tokens, full.at[z], loc.at[0]),
        pltpu.make_async_copy(pool_b, pb_in, loc.at[1]),
        pltpu.make_async_copy(tokens.at[:, pl.ds(chip * 128, 128)], own_tok, loc.at[2]),
        pltpu.make_async_copy(
            pool_a.at[:, :, pl.ds(chip * 128, 128)], pages_a.at[pl.ds(rep * 8, 8)], loc.at[3]
        ),
    ]
    wloads = [
        pltpu.make_async_copy(weight.at[pl.ds(zat(d) * 2048, 2048)], wts.at[d], loc.at[4 + d])
        for d in range(4)
    ]

    barrier = pltpu.get_barrier_semaphore()
    for i in range(1, CHIPS):
        pl.semaphore_signal(barrier, inc=1, device_id=(ahead(i), z), device_id_type=MESH)
    pl.semaphore_signal(barrier, inc=1, device_id=(sibling, z), device_id_type=MESH)
    for d in range(1, 4):
        pl.semaphore_signal(barrier, inc=1, device_id=(rep, zat(d)), device_id_type=MESH)
    for copy in (local[1], local[0], local[2], local[3], wloads[0], wloads[3], wloads[1], wloads[2]):
        copy.start()
    metas[0] = jnp.zeros((8, 128), jnp.int32)
    metas[0, 0:1, 0:32] = list_in[...]
    metas[0, 4:8] = ids_in[...]
    pl.semaphore_wait(barrier, CHIPS - 1 + 4)

    def rows(c):
        return pl.ds(c * 128, 128)

    def z_own(way, c):
        dev = (rep, zat(1 if way == 0 else 3))
        return remote(tokens.at[rows(c)], full.at[z, rows(c)], z_s.at[way, c], z_r.at[way, c], dev)

    def z_relay(way, n):
        c = n + 2 * way
        src = zat(3 if way == 0 else 1)
        dev = (rep, zat(1 if way == 0 else 3))
        part = full.at[src, rows(c)]
        return remote(part, part, z_s.at[way, 4 + n], z_r.at[way, 4 + n], dev)

    def send_meta(i):
        return remote(metas.at[0], metas.at[i], m_s.at[i], m_r.at[i], (ahead(i), z))

    def send_a(i):
        to = ahead(i)
        return remote(
            pool_a.at[:, :, pl.ds((to // 2) * 128, 128)], pages_a.at[pl.ds(rep * 8, 8)],
            a_s.at[i], a_r.at[i], (to, z),
        )

    def send_tok(half, i, to):
        n = half * CHIPS + i
        start = pl.multiple_of((to // 2) * 128, 128)
        return remote(
            tokens.at[pl.ds(half * 256, 256), pl.ds(start, 128)], tok.at[half, i],
            tok_s.at[n], tok_r.at[n], (to, z),
        )

    def send_b(i):
        to = ahead(i)
        return remote(
            pb_send.at[to // 2], pages_b.at[pl.ds(rep * 4, 4)], b_s.at[i], b_r.at[i], (to, z)
        )

    def relay_a(i):
        piece = pages_a.at[pl.ds(behind(i) * 8, 8)]
        return remote(piece, piece, ac_s.at[i], ac_r.at[i], (sibling, z))

    def relay_b(i):
        piece = pages_b.at[pl.ds(behind(i) * 4, 4)]
        return remote(piece, piece, bc_s.at[i], bc_r.at[i], (sibling, z))

    for i in range(1, CHIPS):
        send_a(i).start()
    for n in range(2):
        z_own(0, n).start()
        z_own(1, n + 2).start()
    for i in range(1, CHIPS):
        send_meta(i).start()
    for i in range(1, CHIPS):
        send_tok(0, i, ahead(i)).start()

    local[1].wait()

    @pl.loop(0, 4)
    def _(q):
        for j in range(8):
            block = pb_in[q, :, j * 128 : (j + 1) * 128].astype(F32).T.astype(BF16)
            pb_send[2 * j, q] = block[:64]
            pb_send[2 * j + 1, q] = block[64:]

    pages_b[pl.ds(rep * 4, 4)] = pb_send[chip]

    def base_block(d, first):
        m = zat(d)

        @pl.loop(0, 4)
        def _(n):
            cols = pl.ds(pl.multiple_of(n * 256, 256), 256)
            term = jnp.dot(full[m], wts[d, :, cols], preferred_element_type=F32)
            if first:
                acc[:, cols] = term
            else:
                acc[:, cols] += term

    local[3].wait()
    relay_a(0).start()
    relay_b(0).start()
    local[0].wait()
    wloads[0].wait()
    base_block(0, True)

    for i in range(1, CHIPS):
        send_a(i).wait_recv()
        relay_a(i).start()
        send_tok(1, i, ahead(i)).start()
    for n in range(2):
        z_own(0, n + 2).start()
        z_own(1, n).start()
    for i in range(1, CHIPS):
        send_meta(i).wait_recv()
    smem_copy = pltpu.make_async_copy(metas, smem, loc.at[8])
    smem_copy.start()
    for i in range(CHIPS):
        relay_a(i).wait_recv()
    smem_copy.wait()
    local[2].wait()
    tok[0, 0] = own_tok[:256]
    tok[1, 0] = own_tok[256:]

    def ids_of(i, half):
        own = metas[i]
        first = 4 + 2 * half
        return jnp.concatenate([own[first : first + 1], own[first + 1 : first + 2]], axis=1)

    def by_slot(i, ids, left, right, dims):
        total = jnp.zeros((64, 256), F32)
        for g in range(4):
            got = lax.dot_general(
                left[g * 512 : (g + 1) * 512], right, dims, preferred_element_type=F32
            )
            for s in range(8):
                hit = ids == smem[i, 0, g * 8 + s]
                total = jnp.where(hit, got[s * 64 : (s + 1) * 64], total)
        return total

    def send_px(half, i, dev):
        n = half * CHIPS + i
        rows = pl.ds(0, 32)
        return remote(
            part_send.at[half, i, rows], part_recv.at[half, i, rows], px_s.at[n], px_r.at[n],
            (dev, z),
        )

    def send_py(half, i, dev):
        n = half * CHIPS + i
        rows = pl.ds(32, 32)
        return remote(
            part_send.at[half, i, rows], part_recv.at[half, i, rows], py_s.at[n], py_r.at[n],
            (dev, z),
        )

    def shrink(half):
        @pl.loop(0, CHIPS)
        def _(i):
            @pl.when(i > 0)
            def _():
                send_tok(half, i, rep).wait_recv()

            for s in range(32):
                stage[s * 64 : (s + 1) * 64] = pages_a[table[smem[i, 0, s]]]
            part_send[half, i] = by_slot(i, ids_of(i, half), stage, tok[half, i], NT)

            dx = lookup([o[0] for o in OFFS], i)
            dy = lookup([o[1] for o in OFFS], i)

            @pl.when(dx > 0)
            def _():
                send_px(half, i, rep_at((x + 4 - dx) % 4, y)).start()

            @pl.when(dy > 0)
            def _():
                send_py(half, i, rep_at(x, (y + 4 - dy) % 4)).start()

    shrink(0)
    for n in range(2):
        z_own(0, n).wait_recv()
        z_relay(0, n).start()
        z_own(1, n + 2).wait_recv()
        z_relay(1, n).start()
    shrink(1)

    def send_ex(half, dy):
        n = half * 4 + dy
        dev = rep_at(x, (y + 4 - dy) % 4)
        return remote(mid.at[half, 0, dy], end.at[half, 0, dy], ex_s.at[n], ex_r.at[n], (dev, z))

    def send_ey(half, dx):
        n = half * 4 + dx
        dev = rep_at((x + 4 - dx) % 4, y)
        return remote(mid.at[half, 1, dx], end.at[half, 1, dx], ey_s.at[n], ey_r.at[n], (dev, z))

    def first_sums(half):
        for o in (1, 3, 2, 0):
            for d in range(1, 4):
                send_px(half, OFFS.index((d, o)), rep).wait_recv()
            total = part_send[half, OFFS.index((0, o)), :32]
            for d in range(1, 4):
                total = total + part_recv[half, OFFS.index((d, o)), :32]
            mid[half, 0, o] = total
            if o:
                send_ex(half, o).start()
            for d in range(1, 4):
                send_py(half, OFFS.index((o, d)), rep).wait_recv()
            total = part_send[half, OFFS.index((o, 0)), 32:]
            for d in range(1, 4):
                total = total + part_recv[half, OFFS.index((o, d)), 32:]
            mid[half, 1, o] = total
            if o:
                send_ey(half, o).start()

    def collect(half):
        for axis in range(2):
            total = mid[half, axis, 0]
            for o in (1, 3, 2):
                (send_ey if axis else send_ex)(half, o).wait_recv()
                total = total + end[half, axis, o]
            zsum[half, 2 * axis] = total[:16]
            zsum[half, 2 * axis + 1] = total[16:]

    def send_zsum(half, d):
        to = zat(d)
        n = half * 4 + d
        return remote(zsum.at[half, to], zrecv.at[half, d], zp_s.at[n], zp_r.at[n], (rep, to))

    def start_sums(half):
        for d in (2, 1, 3):
            send_zsum(half, d).start()

    def send_rank(half, i, to):
        n = half * CHIPS + i
        return remote(ranks.at[half, z, 0], ranks.at[half, z, i], k_s.at[n], k_r.at[n], (to, z))

    def pass_rank(half, g, d):
        n = (half * 4 + g) * 4 + d
        part = ranks.at[half, z, pl.ds(g * 4, 4)]
        return remote(part, part, zq_s.at[n], zq_r.at[n], (rep, zat(d)))

    def start_ranks(half):
        for d in range(1, 4):
            send_zsum(half, d).wait_recv()
        ranks[half, z, 0] = (
            zsum[half, z] + zrecv[half, 1] + zrecv[half, 2] + zrecv[half, 3]
        ).astype(BF16)
        for i in range(1, CHIPS):
            send_rank(half, i, ahead(i)).start()

    def pass_ranks(half):
        for g in (3, 2, 1, 0):
            for i in range(max(1, 4 * g), 4 * g + 4):
                send_rank(half, i, rep).wait_recv()
            for d in (2, 1, 3):
                pass_rank(half, g, d).start()

    @pl.loop(0, CHIPS)
    def _(i):
        ids = jnp.concatenate([ids_of(i, 0), ids_of(i, 1)], axis=1)
        odd = jnp.zeros((1, 512), jnp.int32)
        for s in range(32):
            name = smem[i, 0, s]
            page = table[name]
            pair[i, s] = page >> 1
            odd = jnp.where(ids == name, page & 1, odd)
        odds[i] = odd

    first_sums(0)
    collect(0)
    start_sums(0)
    first_sums(1)
    for i in range(1, CHIPS):
        send_b(i).start()
    start_ranks(0)
    collect(1)
    start_sums(1)
    for n in range(2):
        z_own(0, n + 2).wait_recv()
    wloads[3].wait()
    base_block(3, False)
    start_ranks(1)
    pass_ranks(0)
    pass_ranks(1)
    for n in range(2):
        z_own(1, n).wait_recv()
    wloads[1].wait()
    for i in range(1, CHIPS):
        send_b(i).wait_recv()
        relay_b(i).start()
    base_block(1, False)
    for i in range(CHIPS):
        relay_b(i).wait_recv()

    def send_delta(i, dev):
        return remote(delta_send.at[i], delta_recv.at[chip], d_s.at[i], d_r.at[i], (dev, z))

    @pl.loop(0, CHIPS)
    def _(step):
        i = CHIPS - 1 - step
        for s in range(32):
            stage[s * 64 : (s + 1) * 64] = pages_b[pair[i, s]]

        @pl.when(step % 4 == 0)
        def _():
            for half in range(2):
                for d in range(1, 4):
                    pass_rank(half, i // 4, d).wait_recv()

        for half in range(2):
            odd = odds[i, :, half * 256 : (half + 1) * 256]
            vals = jnp.concatenate([ranks[half, q, i] for q in range(4)], axis=0).astype(F32)
            vals = jnp.concatenate(
                [jnp.where(odd == 0, vals, 0.0), jnp.where(odd == 1, vals, 0.0)], axis=0
            ).astype(BF16)
            delta_send[i, half] = by_slot(i, ids_of(i, half), stage, vals, NN).astype(BF16)

        @pl.when(i > 0)
        def _():
            send_delta(i, behind_loop(i)).start()

    delta_recv[chip] = delta_send[0]

    for n in range(2):
        z_relay(0, n).wait_recv()
        z_relay(1, n).wait_recv()
    wloads[2].wait()
    base_block(2, False)

    for i in range(1, CHIPS):
        send_delta(i, rep).wait_recv()
    for half in range(2):

        @pl.loop(0, 8)
        def _(j):
            part = pl.ds(half * 256, 256)
            cols = pl.ds(pl.multiple_of(j * 128, 128), 128)
            block = jnp.concatenate(
                [delta_recv[2 * j, half], delta_recv[2 * j + 1, half]], axis=0
            )
            out[part, cols] = (acc[part, cols] + block.astype(F32).T).astype(BF16)

    for way in range(2):
        for n in range(4):
            z_own(way, n).wait_send()
        for n in range(2):
            z_relay(way, n).wait_send()
    for i in range(1, CHIPS):
        send_a(i).wait_send()
        send_meta(i).wait_send()
        send_b(i).wait_send()
        send_delta(i, rep).wait_send()
        for half in range(2):
            send_tok(half, i, rep).wait_send()
            send_rank(half, i, rep).wait_send()
    for i in range(CHIPS):
        relay_a(i).wait_send()
        relay_b(i).wait_send()
    for half in range(2):
        for i, (dx, dy) in enumerate(OFFS):
            if dx:
                send_px(half, i, rep).wait_send()
            if dy:
                send_py(half, i, rep).wait_send()
        for d in range(1, 4):
            send_ex(half, d).wait_send()
            send_ey(half, d).wait_send()
            send_zsum(half, d).wait_send()
            for g in range(4):
                pass_rank(half, g, d).wait_send()


def per_device(tokens, tok_adapter, requests, owner_table, q_weight, pool_a, pool_b):
    dma = pltpu.SemaphoreType.DMA
    anywhere = pl.BlockSpec(memory_space=pl.ANY)
    vmem = pl.BlockSpec(memory_space=pltpu.VMEM)
    smem = pl.BlockSpec(memory_space=pltpu.SMEM)
    return pl.pallas_call(
        kernel,
        out_shape=jax.ShapeDtypeStruct((512, 1024), BF16),
        in_specs=[anywhere, vmem, vmem, smem, anywhere, anywhere, anywhere],
        out_specs=vmem,
        scratch_shapes=[
            pltpu.VMEM((4, 512, 2048), BF16),
            pltpu.VMEM((4, 2048, 1024), BF16),
            pltpu.VMEM((512, 128), BF16),
            pltpu.VMEM((2, 16, 256, 128), BF16),
            pltpu.VMEM((256, 64, 128), BF16),
            pltpu.VMEM((4, 128, 1024), BF16),
            pltpu.VMEM((16, 4, 64, 128), BF16),
            pltpu.VMEM((128, 64, 128), BF16),
            pltpu.VMEM((16, 8, 128), jnp.int32),
            pltpu.SMEM((16, 8, 128), jnp.int32),
            pltpu.SMEM((16, 32), jnp.int32),
            pltpu.VMEM((16, 1, 512), jnp.int32),
            pltpu.VMEM((2048, 128), BF16),
            pltpu.VMEM((2, 16, 64, 256), F32),
            pltpu.VMEM((2, 16, 64, 256), F32),
            pltpu.VMEM((2, 2, 4, 32, 256), F32),
            pltpu.VMEM((2, 2, 4, 32, 256), F32),
            pltpu.VMEM((2, 4, 16, 256), F32),
            pltpu.VMEM((2, 4, 16, 256), F32),
            pltpu.VMEM((2, 4, 16, 16, 256), BF16),
            pltpu.VMEM((16, 2, 64, 256), BF16),
            pltpu.VMEM((16, 2, 64, 256), BF16),
            pltpu.VMEM((512, 1024), F32),
            dma((2, 6)), dma((2, 6)),
            dma((32,)), dma((32,)),
            dma((16,)), dma((16,)),
            dma((16,)), dma((16,)),
            dma((16,)), dma((16,)),
            dma((16,)), dma((16,)),
            dma((16,)), dma((16,)),
            dma((32,)), dma((32,)),
            dma((32,)), dma((32,)),
            dma((8,)), dma((8,)),
            dma((8,)), dma((8,)),
            dma((8,)), dma((8,)),
            dma((32,)), dma((32,)),
            dma((32,)), dma((32,)),
            dma((16,)), dma((16,)),
            dma((9,)),
        ],
        compiler_params=pltpu.CompilerParams(
            collective_id=1, has_side_effects=True, vmem_limit_bytes=62 * 2**20
        ),
        cost_estimate=pl.CostEstimate(
            flops=20_000_000_000, bytes_accessed=30_000_000, transcendentals=0
        ),
        name="lora_projection",
    )(tokens, tok_adapter.reshape(4, 128), requests, owner_table, q_weight, pool_a, pool_b.reshape(4, 128, 1024))


def solution(mesh):
    in_specs = (
        P("rep", "mp"),
        P("rep"),
        P("rep", None),
        P(),
        P(None, "mp"),
        P("rep", None, "mp"),
        P("rep", None, "mp"),
    )
    out_specs = P("rep", "mp")
    return jax.shard_map(
        per_device, mesh=mesh, in_specs=in_specs, out_specs=out_specs, check_vma=False
    )
```

```python
import jax
import jax.numpy as jnp
from jax import lax
from jax.experimental import pallas as pl
from jax.experimental.pallas import tpu as pltpu
from jax.sharding import PartitionSpec as P

MESH = pl.DeviceIdType.MESH
F32 = jnp.float32
BF16 = jnp.bfloat16

OFFS = (
    (0, 0),
    (1, 0), (3, 0), (0, 1), (0, 3),
    (1, 1), (3, 3), (1, 3), (3, 1),
    (2, 1), (1, 2), (2, 3), (3, 2),
    (2, 0), (0, 2), (2, 2),
)
CHIPS = 16
NT = (((1,), (1,)), ((), ()))
NN = (((1,), (0,)), ((), ()))


def lookup(values, i):
    found = jnp.int32(0)
    for j, value in enumerate(values):
        if value:
            found = found + value * (i == j).astype(jnp.int32)
    return found


def kernel(
    tokens, ids_in, list_in, table, weight, pool_a, pool_b,
    out,
    full, wts, own_tok, tok, pages_a, pb_in, pb_send, pages_b, metas, smem, pair, odds, stage,
    part_send, part_recv, mid, end, zsum, zrecv, ranks, delta_send, delta_recv, acc,
    z_s, z_r, tok_s, tok_r, a_s, a_r, ac_s, ac_r, b_s, b_r, bc_s, bc_r, m_s, m_r,
    px_s, px_r, py_s, py_r, ex_s, ex_r, ey_s, ey_r, zp_s, zp_r, zq_s, zq_r, k_s, k_r, d_s, d_r, loc,
):
    rep = lax.axis_index("rep")
    z = lax.axis_index("mp")
    x, y, core = rep // 8, (rep // 2) % 4, rep % 2
    chip = x * 4 + y

    def rep_at(cx, cy):
        return (cx * 4 + cy) * 2 + core

    def ahead(i):
        dx, dy = OFFS[i]
        return (((x + dx) % 4) * 4 + (y + dy) % 4) * 2 + core

    def behind(i):
        dx, dy = OFFS[i]
        return (((x + 4 - dx) % 4) * 4 + (y + 4 - dy) % 4) * 2 + core

    def ahead_loop(i):
        dx = lookup([o[0] for o in OFFS], i)
        dy = lookup([o[1] for o in OFFS], i)
        return (((x + dx) % 4) * 4 + (y + dy) % 4) * 2 + core

    def behind_loop(i):
        dx = lookup([o[0] for o in OFFS], i)
        dy = lookup([o[1] for o in OFFS], i)
        return (((x + 4 - dx) % 4) * 4 + (y + 4 - dy) % 4) * 2 + core

    def zat(d):
        return (z + d) % 4

    sibling = rep + 1 - 2 * core

    def remote(src, dst, ss, rs, dev):
        return pltpu.make_async_remote_copy(
            src_ref=src, dst_ref=dst, send_sem=ss, recv_sem=rs, device_id=dev, device_id_type=MESH
        )

    local = [
        pltpu.make_async_copy(tokens, full.at[z], loc.at[0]),
        pltpu.make_async_copy(pool_b, pb_in, loc.at[1]),
        pltpu.make_async_copy(tokens.at[:, pl.ds(chip * 128, 128)], own_tok, loc.at[2]),
        pltpu.make_async_copy(
            pool_a.at[:, :, pl.ds(chip * 128, 128)], pages_a.at[pl.ds(rep * 8, 8)], loc.at[3]
        ),
    ]
    wloads = [
        pltpu.make_async_copy(weight.at[pl.ds(zat(d) * 2048, 2048)], wts.at[d], loc.at[4 + d])
        for d in range(4)
    ]

    barrier = pltpu.get_barrier_semaphore()
    for i in range(1, CHIPS):
        pl.semaphore_signal(barrier, inc=1, device_id=(ahead(i), z), device_id_type=MESH)
    pl.semaphore_signal(barrier, inc=1, device_id=(sibling, z), device_id_type=MESH)
    for d in range(1, 4):
        pl.semaphore_signal(barrier, inc=1, device_id=(rep, zat(d)), device_id_type=MESH)
    for copy in (local[1], local[0], local[2], local[3], wloads[0], wloads[3], wloads[1], wloads[2]):
        copy.start()
    metas[0] = jnp.zeros((8, 128), jnp.int32)
    metas[0, 0:1, 0:32] = list_in[...]
    metas[0, 4:8] = ids_in[...]
    pl.semaphore_wait(barrier, CHIPS - 1 + 4)

    def rows(c):
        return pl.ds(c * 128, 128)

    def z_own(way, c):
        dev = (rep, zat(1 if way == 0 else 3))
        return remote(tokens.at[rows(c)], full.at[z, rows(c)], z_s.at[way, c], z_r.at[way, c], dev)

    def z_relay(way, n):
        c = n + 2 * way
        src = zat(3 if way == 0 else 1)
        dev = (rep, zat(1 if way == 0 else 3))
        part = full.at[src, rows(c)]
        return remote(part, part, z_s.at[way, 4 + n], z_r.at[way, 4 + n], dev)

    def send_meta(i):
        return remote(metas.at[0], metas.at[i], m_s.at[i], m_r.at[i], (ahead(i), z))

    def send_a(i):
        to = ahead(i)
        return remote(
            pool_a.at[:, :, pl.ds((to // 2) * 128, 128)], pages_a.at[pl.ds(rep * 8, 8)],
            a_s.at[i], a_r.at[i], (to, z),
        )

    def send_tok(half, i, to):
        n = half * CHIPS + i
        start = pl.multiple_of((to // 2) * 128, 128)
        return remote(
            tokens.at[pl.ds(half * 256, 256), pl.ds(start, 128)], tok.at[half, i],
            tok_s.at[n], tok_r.at[n], (to, z),
        )

    def send_b(i):
        to = ahead(i)
        return remote(
            pb_send.at[to // 2], pages_b.at[pl.ds(rep * 4, 4)], b_s.at[i], b_r.at[i], (to, z)
        )

    def relay_a(i):
        piece = pages_a.at[pl.ds(behind(i) * 8, 8)]
        return remote(piece, piece, ac_s.at[i], ac_r.at[i], (sibling, z))

    def relay_b(i):
        piece = pages_b.at[pl.ds(behind(i) * 4, 4)]
        return remote(piece, piece, bc_s.at[i], bc_r.at[i], (sibling, z))

    for i in range(1, CHIPS):
        send_a(i).start()
    for n in range(2):
        z_own(0, n).start()
        z_own(1, n + 2).start()
    for i in range(1, CHIPS):
        send_meta(i).start()
    for i in range(1, CHIPS):
        send_tok(0, i, ahead(i)).start()

    local[1].wait()

    @pl.loop(0, 4)
    def _(q):
        for j in range(8):
            block = pb_in[q, :, j * 128 : (j + 1) * 128].astype(F32).T.astype(BF16)
            pb_send[2 * j, q] = block[:64]
            pb_send[2 * j + 1, q] = block[64:]

    pages_b[pl.ds(rep * 4, 4)] = pb_send[chip]

    def base_block(d, first):
        m = zat(d)

        @pl.loop(0, 4)
        def _(n):
            cols = pl.ds(pl.multiple_of(n * 256, 256), 256)
            term = jnp.dot(full[m], wts[d, :, cols], preferred_element_type=F32)
            if first:
                acc[:, cols] = term
            else:
                acc[:, cols] += term

    local[3].wait()
    relay_a(0).start()
    relay_b(0).start()
    local[0].wait()
    wloads[0].wait()
    base_block(0, True)

    for i in range(1, CHIPS):
        send_a(i).wait_recv()
        relay_a(i).start()
        send_tok(1, i, ahead(i)).start()
    for n in range(2):
        z_own(0, n + 2).start()
        z_own(1, n).start()
    for i in range(1, CHIPS):
        send_meta(i).wait_recv()
    smem_copy = pltpu.make_async_copy(metas, smem, loc.at[8])
    smem_copy.start()
    for i in range(CHIPS):
        relay_a(i).wait_recv()
    smem_copy.wait()
    local[2].wait()
    tok[0, 0] = own_tok[:256]
    tok[1, 0] = own_tok[256:]

    def ids_of(i, half):
        own = metas[i]
        first = 4 + 2 * half
        return jnp.concatenate([own[first : first + 1], own[first + 1 : first + 2]], axis=1)

    def by_slot(i, ids, left, right, dims):
        total = jnp.zeros((64, 256), F32)
        for g in range(4):
            got = lax.dot_general(
                left[g * 512 : (g + 1) * 512], right, dims, preferred_element_type=F32
            )
            for s in range(8):
                hit = ids == smem[i, 0, g * 8 + s]
                total = jnp.where(hit, got[s * 64 : (s + 1) * 64], total)
        return total

    def send_px(half, i, dev):
        n = half * CHIPS + i
        rows = pl.ds(0, 32)
        return remote(
            part_send.at[half, i, rows], part_recv.at[half, i, rows], px_s.at[n], px_r.at[n],
            (dev, z),
        )

    def send_py(half, i, dev):
        n = half * CHIPS + i
        rows = pl.ds(32, 32)
        return remote(
            part_send.at[half, i, rows], part_recv.at[half, i, rows], py_s.at[n], py_r.at[n],
            (dev, z),
        )

    def shrink(half):
        @pl.loop(0, CHIPS)
        def _(i):
            @pl.when(i > 0)
            def _():
                send_tok(half, i, rep).wait_recv()

            for s in range(32):
                stage[s * 64 : (s + 1) * 64] = pages_a[table[smem[i, 0, s]]]
            part_send[half, i] = by_slot(i, ids_of(i, half), stage, tok[half, i], NT)

            dx = lookup([o[0] for o in OFFS], i)
            dy = lookup([o[1] for o in OFFS], i)

            @pl.when(dx > 0)
            def _():
                send_px(half, i, rep_at((x + 4 - dx) % 4, y)).start()

            @pl.when(dy > 0)
            def _():
                send_py(half, i, rep_at(x, (y + 4 - dy) % 4)).start()

    shrink(0)
    for n in range(2):
        z_own(0, n).wait_recv()
        z_relay(0, n).start()
        z_own(1, n + 2).wait_recv()
        z_relay(1, n).start()
    shrink(1)

    def send_ex(half, dy):
        n = half * 4 + dy
        dev = rep_at(x, (y + 4 - dy) % 4)
        return remote(mid.at[half, 0, dy], end.at[half, 0, dy], ex_s.at[n], ex_r.at[n], (dev, z))

    def send_ey(half, dx):
        n = half * 4 + dx
        dev = rep_at((x + 4 - dx) % 4, y)
        return remote(mid.at[half, 1, dx], end.at[half, 1, dx], ey_s.at[n], ey_r.at[n], (dev, z))

    def first_sums(half):
        for o in (1, 3, 2, 0):
            for d in range(1, 4):
                send_px(half, OFFS.index((d, o)), rep).wait_recv()
            total = part_send[half, OFFS.index((0, o)), :32]
            for d in range(1, 4):
                total = total + part_recv[half, OFFS.index((d, o)), :32]
            mid[half, 0, o] = total
            if o:
                send_ex(half, o).start()
            for d in range(1, 4):
                send_py(half, OFFS.index((o, d)), rep).wait_recv()
            total = part_send[half, OFFS.index((o, 0)), 32:]
            for d in range(1, 4):
                total = total + part_recv[half, OFFS.index((o, d)), 32:]
            mid[half, 1, o] = total
            if o:
                send_ey(half, o).start()

    def collect(half):
        for axis in range(2):
            total = mid[half, axis, 0]
            for o in (1, 3, 2):
                (send_ey if axis else send_ex)(half, o).wait_recv()
                total = total + end[half, axis, o]
            zsum[half, 2 * axis] = total[:16]
            zsum[half, 2 * axis + 1] = total[16:]

    def send_zsum(half, d):
        to = zat(d)
        n = half * 4 + d
        return remote(zsum.at[half, to], zrecv.at[half, d], zp_s.at[n], zp_r.at[n], (rep, to))

    def start_sums(half):
        for d in (2, 1, 3):
            send_zsum(half, d).start()

    def send_rank(half, i, to):
        n = half * CHIPS + i
        return remote(ranks.at[half, z, 0], ranks.at[half, z, i], k_s.at[n], k_r.at[n], (to, z))

    def pass_rank(half, g, d):
        n = (half * 4 + g) * 4 + d
        part = ranks.at[half, z, pl.ds(g * 4, 4)]
        return remote(part, part, zq_s.at[n], zq_r.at[n], (rep, zat(d)))

    def start_ranks(half):
        for d in range(1, 4):
            send_zsum(half, d).wait_recv()
        ranks[half, z, 0] = (
            zsum[half, z] + zrecv[half, 1] + zrecv[half, 2] + zrecv[half, 3]
        ).astype(BF16)
        for i in range(CHIPS - 1, 0, -1):
            send_rank(half, i, ahead(i)).start()

    def pass_ranks(half):
        for g in (3, 2, 1, 0):
            for i in range(max(1, 4 * g), 4 * g + 4):
                send_rank(half, i, rep).wait_recv()
            for d in (2, 1, 3):
                pass_rank(half, g, d).start()

    @pl.loop(0, CHIPS)
    def _(i):
        ids = jnp.concatenate([ids_of(i, 0), ids_of(i, 1)], axis=1)
        odd = jnp.zeros((1, 512), jnp.int32)
        for s in range(32):
            name = smem[i, 0, s]
            page = table[name]
            pair[i, s] = page >> 1
            odd = jnp.where(ids == name, page & 1, odd)
        odds[i] = odd

    first_sums(0)
    collect(0)
    start_sums(0)
    first_sums(1)
    for i in range(1, CHIPS):
        send_b(i).start()
    start_ranks(0)
    collect(1)
    start_sums(1)
    for n in range(2):
        z_own(0, n + 2).wait_recv()
    wloads[3].wait()
    base_block(3, False)
    start_ranks(1)
    pass_ranks(0)
    pass_ranks(1)
    for n in range(2):
        z_own(1, n).wait_recv()
    wloads[1].wait()
    for i in range(1, CHIPS):
        send_b(i).wait_recv()
        relay_b(i).start()
    base_block(1, False)
    for i in range(CHIPS):
        relay_b(i).wait_recv()

    def send_delta(i, dev):
        return remote(delta_send.at[i], delta_recv.at[chip], d_s.at[i], d_r.at[i], (dev, z))

    @pl.loop(0, CHIPS)
    def _(step):
        i = CHIPS - 1 - step
        for s in range(32):
            stage[s * 64 : (s + 1) * 64] = pages_b[pair[i, s]]

        @pl.when(step % 4 == 0)
        def _():
            for half in range(2):
                for d in range(1, 4):
                    pass_rank(half, i // 4, d).wait_recv()

        for half in range(2):
            odd = odds[i, :, half * 256 : (half + 1) * 256]
            vals = jnp.concatenate([ranks[half, q, i] for q in range(4)], axis=0).astype(F32)
            vals = jnp.concatenate(
                [jnp.where(odd == 0, vals, 0.0), jnp.where(odd == 1, vals, 0.0)], axis=0
            ).astype(BF16)
            delta_send[i, half] = by_slot(i, ids_of(i, half), stage, vals, NN).astype(BF16)

        @pl.when(i > 0)
        def _():
            send_delta(i, behind_loop(i)).start()

    delta_recv[chip] = delta_send[0]

    for n in range(2):
        z_relay(0, n).wait_recv()
        z_relay(1, n).wait_recv()
    wloads[2].wait()
    base_block(2, False)

    for i in range(1, CHIPS):
        send_delta(i, rep).wait_recv()
    for half in range(2):

        @pl.loop(0, 8)
        def _(j):
            part = pl.ds(half * 256, 256)
            cols = pl.ds(pl.multiple_of(j * 128, 128), 128)
            block = jnp.concatenate(
                [delta_recv[2 * j, half], delta_recv[2 * j + 1, half]], axis=0
            )
            out[part, cols] = (acc[part, cols] + block.astype(F32).T).astype(BF16)

    for way in range(2):
        for n in range(4):
            z_own(way, n).wait_send()
        for n in range(2):
            z_relay(way, n).wait_send()
    for i in range(1, CHIPS):
        send_a(i).wait_send()
        send_meta(i).wait_send()
        send_b(i).wait_send()
        send_delta(i, rep).wait_send()
        for half in range(2):
            send_tok(half, i, rep).wait_send()
            send_rank(half, i, rep).wait_send()
    for i in range(CHIPS):
        relay_a(i).wait_send()
        relay_b(i).wait_send()
    for half in range(2):
        for i, (dx, dy) in enumerate(OFFS):
            if dx:
                send_px(half, i, rep).wait_send()
            if dy:
                send_py(half, i, rep).wait_send()
        for d in range(1, 4):
            send_ex(half, d).wait_send()
            send_ey(half, d).wait_send()
            send_zsum(half, d).wait_send()
            for g in range(4):
                pass_rank(half, g, d).wait_send()


def per_device(tokens, tok_adapter, requests, owner_table, q_weight, pool_a, pool_b):
    dma = pltpu.SemaphoreType.DMA
    anywhere = pl.BlockSpec(memory_space=pl.ANY)
    vmem = pl.BlockSpec(memory_space=pltpu.VMEM)
    smem = pl.BlockSpec(memory_space=pltpu.SMEM)
    return pl.pallas_call(
        kernel,
        out_shape=jax.ShapeDtypeStruct((512, 1024), BF16),
        in_specs=[anywhere, vmem, vmem, smem, anywhere, anywhere, anywhere],
        out_specs=vmem,
        scratch_shapes=[
            pltpu.VMEM((4, 512, 2048), BF16),
            pltpu.VMEM((4, 2048, 1024), BF16),
            pltpu.VMEM((512, 128), BF16),
            pltpu.VMEM((2, 16, 256, 128), BF16),
            pltpu.VMEM((256, 64, 128), BF16),
            pltpu.VMEM((4, 128, 1024), BF16),
            pltpu.VMEM((16, 4, 64, 128), BF16),
            pltpu.VMEM((128, 64, 128), BF16),
            pltpu.VMEM((16, 8, 128), jnp.int32),
            pltpu.SMEM((16, 8, 128), jnp.int32),
            pltpu.SMEM((16, 32), jnp.int32),
            pltpu.VMEM((16, 1, 512), jnp.int32),
            pltpu.VMEM((2048, 128), BF16),
            pltpu.VMEM((2, 16, 64, 256), F32),
            pltpu.VMEM((2, 16, 64, 256), F32),
            pltpu.VMEM((2, 2, 4, 32, 256), F32),
            pltpu.VMEM((2, 2, 4, 32, 256), F32),
            pltpu.VMEM((2, 4, 16, 256), F32),
            pltpu.VMEM((2, 4, 16, 256), F32),
            pltpu.VMEM((2, 4, 16, 16, 256), BF16),
            pltpu.VMEM((16, 2, 64, 256), BF16),
            pltpu.VMEM((16, 2, 64, 256), BF16),
            pltpu.VMEM((512, 1024), F32),
            dma((2, 6)), dma((2, 6)),
            dma((32,)), dma((32,)),
            dma((16,)), dma((16,)),
            dma((16,)), dma((16,)),
            dma((16,)), dma((16,)),
            dma((16,)), dma((16,)),
            dma((16,)), dma((16,)),
            dma((32,)), dma((32,)),
            dma((32,)), dma((32,)),
            dma((8,)), dma((8,)),
            dma((8,)), dma((8,)),
            dma((8,)), dma((8,)),
            dma((32,)), dma((32,)),
            dma((32,)), dma((32,)),
            dma((16,)), dma((16,)),
            dma((9,)),
        ],
        compiler_params=pltpu.CompilerParams(
            collective_id=1, has_side_effects=True, vmem_limit_bytes=62 * 2**20
        ),
        cost_estimate=pl.CostEstimate(
            flops=20_000_000_000, bytes_accessed=30_000_000, transcendentals=0
        ),
        name="lora_projection",
    )(tokens, tok_adapter.reshape(4, 128), requests, owner_table, q_weight, pool_a, pool_b.reshape(4, 128, 1024))


def solution(mesh):
    in_specs = (
        P("rep", "mp"),
        P("rep"),
        P("rep", None),
        P(),
        P(None, "mp"),
        P("rep", None, "mp"),
        P("rep", None, "mp"),
    )
    out_specs = P("rep", "mp")
    return jax.shard_map(
        per_device, mesh=mesh, in_specs=in_specs, out_specs=out_specs, check_vma=False
    )
```
